256 devices in a mesh: expert: 64 (over y, z, core), hidden: 4 (over x).
Axes of the slice: x: 4, y: 4, z: 8, core: 2. Of those that a mesh axis runs over, the one named last changes fastest.
Arguments:
- tokens: float32 [8192, 2048], P('expert', 'hidden'), may hold values from -6 to 6
- route_first: int32 [8192, 1], P('expert'), may hold values from 0 to 63; in each aligned block of 128 rows (0 to 127, 128 to 255, ...) at most 4 rows name the same one
- route_second: int32 [8192, 1], P('expert'), may hold values from 0 to 63; in each aligned block of 128 rows (0 to 127, 128 to 255, ...) at most 4 rows name the same one
- route_third: int32 [8192, 1], P('expert'), may hold values from 0 to 63; in each aligned block of 128 rows (0 to 127, 128 to 255, ...) at most 4 rows name the same one
- gate_weight: bfloat16 [64, 2048, 1024], P('expert', None, 'hidden'), may hold values from -0.125 to 0.125
- up_weight: bfloat16 [64, 2048, 1024], P('expert', None, 'hidden'), may hold values from -0.125 to 0.125
- down_weight: bfloat16 [64, 1024, 2048], P('expert', 'hidden'), may hold values from -0.1875 to 0.1875
- cotangent: float32 [8192, 2048], P('expert', 'hidden'), may hold values from -6 to 6
Outputs:
- grad_tokens: float32 [8192, 2048], P('expert', 'hidden')
- grad_gate: bfloat16 [64, 2048, 1024], P('expert', None, 'hidden')
- grad_up: bfloat16 [64, 2048, 1024], P('expert', None, 'hidden')
- grad_down: bfloat16 [64, 1024, 2048], P('expert', 'hidden')
The draws below stay inside these ranges and needn't reach their ends.
Inputs may be any that keep to these rules, and one draw needn't show every extreme that they name: `route_first`: in the rows of one index of expert, no expert is named by more than 4 tokens in one visit, a bound that some block reaches; every expert is named somewhere. `route_second`: as for route_first. `route_third`: as for route_first.
All inputs are finite; a program needn't handle non-finite values.
Results may differ from the reference program's by a relative error of at most 0.024.
Values may be sent and summed in bfloat16 or wider, within the bound.
A program may use at most 64 MiB of HBM per device.

```python
import math
import jax
import jax.numpy as jnp
import numpy as np
from jax import lax

D = 2048
FF = 1024
TOK_DEV = 128
EXPERTS = 64
TOKENS = 8192
CAP = 4
EXPERT_ROWS = 256
N_EXPERT = 64


def steps_of(rng, shape, shards, least, high):
    factor_of, own = 1.0, jax.random.fold_in(rng, 6)
    for position, parts in shards:
        steps = jnp.exp(jax.random.uniform(jax.random.fold_in(own, position), (parts,), jnp.float32, least / len(shards), high / len(shards)))
        factor_of = factor_of * jnp.repeat(steps, shape[position] // parts).reshape([-1 if axis == position else 1 for axis in range(len(shape))])
    return factor_of


def deal_out(own_key, own, number, rows, count, top, most, lean):
    sequence = jax.random.permutation(own_key, count)
    crowded, common = load_shares(count, rows * top, most, lean, True), load_shares(count, rows * top, most, lean, False)
    places = jnp.arange(count)

    def named(sizes, rotation):
        used = int((sizes > 0).sum())
        fixed = max(1, used // 4)
        shifted = fixed + (places - fixed + rotation * (used - fixed)) % max(1, count - fixed)
        return jnp.zeros((count,), jnp.int32).at[sequence[jnp.where(places < fixed, places, shifted)]].set(jnp.asarray(sizes, jnp.int32))

    sizes = jnp.where(number % 4 == 0, named(crowded, number // 4), named(common, number - number // 4 - 1))
    mixed = jax.random.permutation(jax.random.fold_in(own, 3), count)
    giver, sink = mixed[0:count // 2 * 2:2], mixed[1:count // 2 * 2:2]
    margin = jnp.minimum(sizes[giver] - 1, most - sizes[sink]) // 2
    margin = jnp.where((giver == sequence[0]) | (sink == sequence[0]) | (sizes[sink] == 0), 0, jnp.maximum(margin, 0))
    shifted = jax.random.randint(jax.random.fold_in(own, 4), (count // 2,), 0, 1 << 20) % (margin + 1)
    sizes = sizes.at[giver].add(-shifted).at[sink].add(shifted)
    labels = jnp.searchsorted(jnp.cumsum(sizes), jnp.arange(rows * top), side="right").astype(jnp.int32)
    grid = labels.reshape(top, rows).T
    grid = grid[jax.random.permutation(jax.random.fold_in(own, 1), rows)]
    rotation = jax.random.randint(jax.random.fold_in(own, 2), (rows, 1), 0, top)
    return jnp.take_along_axis(grid, (jnp.arange(top)[None, :] + rotation) % top, axis=1)


def load_shares(count, total, limit, lean, full):
    portions = [(1 << 20) // math.isqrt(grade ** lean) + 1 for grade in range(1, count + 1)]
    largest = limit if full else min(limit, max(-(-total // count), total * portions[0] // sum(portions)))
    least = 1 if total - largest >= count - 1 else 0
    holding, rest = [largest] + [least] * (count - 1), total - largest - least * (count - 1)
    while rest > 0:
        candidates = [i for i in range(1, count) if holding[i] < largest] or [i for i in range(1, count) if holding[i] < limit]
        pool, budget = sum([portions[i] for i in candidates]), rest
        for i in candidates:
            extra = min(limit - holding[i], max(1, budget * portions[i] // pool), rest)
            holding[i] = holding[i] + extra
            rest = rest - extra
    return np.array(holding)


def scatter_about(stream_key, dims, deviation, reach, cuts=(), kind=jnp.bfloat16):
    entries = jax.random.normal(stream_key, dims, jnp.float32) * deviation
    if len(cuts) > 0:
        entries = steps_of(stream_key, dims, cuts, -0.22, 0.18) * entries
    return jnp.clip(entries, min=-reach, max=reach).astype(kind)


def setup_inputs(seed: int = 0) -> dict:
    streams_of = jax.random.split(jax.random.key(seed), 9)
    tokens = scatter_about(streams_of[0], (TOKENS, D), 1.0, 6.0, ((0, 64), (1, 4)), jnp.float32)
    route_first_keys = jax.random.split(jax.random.fold_in(streams_of[1], 1), TOKENS // TOK_DEV)
    route_first_turns = jax.random.permutation(jax.random.fold_in(streams_of[1], 3), TOKENS // TOK_DEV)
    route_first = jax.vmap(lambda own, number: deal_out(jax.random.fold_in(streams_of[1], 2), own, number, TOK_DEV, EXPERTS, 1, CAP, 2))(route_first_keys, route_first_turns).reshape((TOKENS, 1))
    route_second_keys = jax.random.split(jax.random.fold_in(streams_of[2], 1), TOKENS // TOK_DEV)
    route_second_turns = jax.random.permutation(jax.random.fold_in(streams_of[2], 3), TOKENS // TOK_DEV)
    route_second = jax.vmap(lambda own, number: deal_out(jax.random.fold_in(streams_of[2], 2), own, number, TOK_DEV, EXPERTS, 1, CAP, 2))(route_second_keys, route_second_turns).reshape((TOKENS, 1))
    route_third_keys = jax.random.split(jax.random.fold_in(streams_of[3], 1), TOKENS // TOK_DEV)
    route_third_turns = jax.random.permutation(jax.random.fold_in(streams_of[3], 3), TOKENS // TOK_DEV)
    route_third = jax.vmap(lambda own, number: deal_out(jax.random.fold_in(streams_of[3], 2), own, number, TOK_DEV, EXPERTS, 1, CAP, 2))(route_third_keys, route_third_turns).reshape((TOKENS, 1))
    gate_weight = scatter_about(streams_of[4], (EXPERTS, D, FF), D ** -0.5, 0.125, ((0, 64), (2, 4)))
    up_weight = scatter_about(streams_of[5], (EXPERTS, D, FF), D ** -0.5, 0.125, ((0, 64), (2, 4)))
    down_weight = scatter_about(streams_of[6], (EXPERTS, FF, D), FF ** -0.5, 0.1875, ((0, 64), (1, 4)))
    cotangent = scatter_about(streams_of[7], (TOKENS, D), 1.0, 6.0, ((0, 64), (1, 4)), jnp.float32)
    return {"tokens": tokens, "route_first": route_first, "route_second": route_second, "route_third": route_third, "gate_weight": gate_weight, "up_weight": up_weight, "down_weight": down_weight, "cotangent": cotangent}


def slot_index(route):
    owner_ids = route[:, 0].astype(jnp.int32)
    onehot = (owner_ids[:, None] == jnp.arange(EXPERTS, dtype=jnp.int32)[None, :]).astype(jnp.int32)
    blocks = onehot.reshape(N_EXPERT, TOK_DEV, EXPERTS)
    before = jnp.cumsum(blocks, axis=1) - blocks
    ranks = jnp.sum(before * blocks, axis=2).reshape(-1)
    source = jnp.arange(TOKENS, dtype=jnp.int32) // TOK_DEV
    return (owner_ids * EXPERT_ROWS + source * CAP + ranks).astype(jnp.int32)


def dispatch(rows, slots):
    table = jnp.zeros((EXPERTS * EXPERT_ROWS, D), rows.dtype).at[slots].set(rows)
    return table.reshape(EXPERTS, EXPERT_ROWS, D)


def combine(table, slots):
    return table.reshape(EXPERTS * EXPERT_ROWS, D)[slots]


def front(packed):
    inputs, gate_w, lift_w = packed
    return (jnp.dot(inputs, gate_w, preferred_element_type=jnp.float32),
            jnp.dot(inputs, lift_w, preferred_element_type=jnp.float32))


def project(packed):
    hidden, down_w = packed
    return jnp.dot(hidden, down_w, preferred_element_type=jnp.float32)


def backward_expert(packed):
    inputs, gate, lifted, grad_rows, gate_w, lift_w, down_w = packed
    sigma = jax.nn.sigmoid(gate)
    swish = gate * sigma
    hidden = (swish * lifted).astype(jnp.bfloat16)
    grad_down = jnp.dot(hidden.T, grad_rows, preferred_element_type=jnp.float32)
    grad_hidden = jnp.dot(grad_rows, down_w.T, preferred_element_type=jnp.float32)
    grad_gate = (grad_hidden * lifted * sigma * (1.0 + gate * (1.0 - sigma))).astype(jnp.bfloat16)
    grad_lift = (grad_hidden * swish).astype(jnp.bfloat16)
    weight_gate = jnp.dot(inputs.T, grad_gate, preferred_element_type=jnp.float32)
    weight_lift = jnp.dot(inputs.T, grad_lift, preferred_element_type=jnp.float32)
    grad_inputs = (jnp.dot(grad_gate, gate_w.T, preferred_element_type=jnp.float32)
                   + jnp.dot(grad_lift, lift_w.T, preferred_element_type=jnp.float32))
    return weight_gate, weight_lift, grad_down, grad_inputs


def reference(tokens, route_first, route_second, route_third, gate_weight, up_weight, down_weight, cotangent):
    slot_list = [slot_index(route_first), slot_index(route_second), slot_index(route_third)]
    state = tokens
    saved = []
    for visit in range(3):
        slots = slot_list[visit]
        inputs = dispatch(state.astype(jnp.bfloat16), slots)
        gate, lifted = lax.map(front, (inputs, gate_weight, up_weight))
        saved.append((inputs, gate, lifted))
        if visit < 2:
            hidden = (jax.nn.sigmoid(gate) * gate * lifted).astype(jnp.bfloat16)
            outputs = lax.map(project, (hidden, down_weight))
            state = state + combine(outputs, slots)
    grad = cotangent
    total_gate = jnp.zeros((EXPERTS, D, FF), jnp.float32)
    total_lift = jnp.zeros((EXPERTS, D, FF), jnp.float32)
    total_down = jnp.zeros((EXPERTS, FF, D), jnp.float32)
    for visit in (2, 1, 0):
        slots = slot_list[visit]
        inputs, gate, lifted = saved[visit]
        grad_rows = dispatch(grad.astype(jnp.bfloat16), slots)
        weight_gate, weight_lift, grad_down, grad_inputs = lax.map(
            backward_expert, (inputs, gate, lifted, grad_rows, gate_weight, up_weight, down_weight))
        total_gate = total_gate + weight_gate
        total_lift = total_lift + weight_lift
        total_down = total_down + grad_down
        grad = grad + combine(grad_inputs, slots)
    return (grad, total_gate.astype(jnp.bfloat16), total_lift.astype(jnp.bfloat16),
            total_down.astype(jnp.bfloat16))
```

```python
import jax
import jax.numpy as jnp
from jax import lax
from jax.experimental import pallas as pl
from jax.experimental.pallas import tpu as pltpu
from jax.sharding import PartitionSpec as P

MESH = pl.DeviceIdType.MESH
F32 = jnp.float32
BF16 = jnp.bfloat16
EXPERTS = 64
RANKS = 4
HIDDEN = 4
VMEM = pltpu.VMEM


def dot(a, b):
    return jnp.dot(a, b, preferred_element_type=F32)


def contract_last(a, b):
    return lax.dot_general(a, b, (((1,), (1,)), ((), ())), preferred_element_type=F32)


def contract_first(a, b):
    return lax.dot_general(a, b, (((0,), (0,)), ((), ())), preferred_element_type=F32)


def exact_ones(condition):
    return jnp.where(condition, 1.0, 0.0).astype(BF16)


def kernel(
    tok, cot, krow, kcol, gate_hbm, up_hbm, down_hbm,
    out_tok, out_gate, out_up, out_down,
    wg, wu, wd, place, fetch, perm, perm_t, sent, got, rows_of, part_out, relayed, summed,
    gate, lift, hid, dgate, dup, own, acc_gate, acc_up, acc_down, res_gate, res_up, res_down, state, grad,
    sem_w, sem_send, sem_got, sem_xs, sem_xr, sem_ys, sem_yr,
):
    me = lax.axis_index("expert")
    h = lax.axis_index("hidden")
    right, left, across = lax.rem(h + 1, HIDDEN), lax.rem(h + 3, HIDDEN), lax.rem(h + 2, HIDDEN)

    loads = [
        pltpu.make_async_copy(gate_hbm, wg, sem_w.at[0]),
        pltpu.make_async_copy(up_hbm, wu, sem_w.at[1]),
    ] + [
        pltpu.make_async_copy(down_hbm.at[:, pl.ds(k * 512, 512)], wd.at[k], sem_w.at[2 + k])
        for k in range(HIDDEN)
    ]
    for load in loads:
        load.start()

    barrier = pltpu.get_barrier_semaphore()

    def greet(j, carry):
        pl.semaphore_signal(barrier, inc=1, device_id=(lax.rem(me + j, EXPERTS), h), device_id_type=MESH)
        return carry

    lax.fori_loop(1, EXPERTS, greet, 0)
    for side in (left, right):
        pl.semaphore_signal(barrier, inc=1, device_id=(me, side), device_id_type=MESH)

    def build(visit):
        def step(g, carry):
            rows = pl.ds(pl.multiple_of(g * 256, 256), 256)
            numbers = lax.broadcasted_iota(jnp.int32, (256, 512), 0) + g * 256
            place[visit, rows, :] = exact_ones(numbers == krow[visit])
            half = pl.ds(pl.multiple_of(g * 128, 128), 128)
            across_lanes = lax.broadcasted_iota(jnp.int32, (128, 1024), 1)
            fetch[visit, half, :] = exact_ones(across_lanes == kcol[visit, half, :])
            return carry

        lax.fori_loop(0, 4, step, 0)

    def image(slot_number):
        c, s = slot_number // 64, slot_number % 64
        return (s // 4) * 16 + c * 4 + s % 4

    first = lax.broadcasted_iota(jnp.int32, (256, 256), 0)
    second = lax.broadcasted_iota(jnp.int32, (256, 256), 1)
    perm[...] = exact_ones(second == image(first))
    perm_t[...] = exact_ones(first == image(second))
    build(0)
    state[...] = tok[...]
    grad[...] = cot[...]
    pl.semaphore_wait(barrier, EXPERTS + 1)

    pending = []

    def send_group(n, g, forward):
        def go(j, carry):
            rows = pl.ds(pl.multiple_of(j * 16, 16), 16)
            step = j if forward else EXPERTS - j
            pltpu.make_async_remote_copy(
                src_ref=sent.at[n, rows], dst_ref=got.at[n, rows],
                send_sem=sem_send.at[n], recv_sem=sem_got.at[n],
                device_id=(lax.rem(me + step, EXPERTS), h), device_id_type=MESH,
            ).start()
            return carry

        lax.fori_loop(max(1, g * 16), g * 16 + 16, go, 0)

    def whole(n):
        rows = pl.ds(16, (EXPERTS - 1) * 16)
        return pltpu.make_async_remote_copy(
            src_ref=sent.at[n, rows], dst_ref=got.at[n, rows],
            send_sem=sem_send.at[n], recv_sem=sem_got.at[n],
            device_id=(lax.rem(me + 1, EXPERTS), h), device_id_type=MESH,
        )

    def exchanged(n):
        whole(n).wait_recv()
        pending.append(whole(n))

    def dispatch(n, visit, values):
        values = values.astype(BF16)
        stacked = jnp.concatenate([values[:, c * 128 : (c + 1) * 128] for c in range(4)], axis=0)
        for g in range(4):
            rows = pl.ds(g * 256, 256)
            sent[n, rows, :] = dot(place[visit, rows, :], stacked).astype(BF16)
            send_group(n, g, True)
        got[n, 0:16, :] = sent[n, 0:16, :]

    def hand(ref_from, ref_to, s, r, side):
        copy = pltpu.make_async_remote_copy(
            src_ref=ref_from, dst_ref=ref_to, send_sem=s, recv_sem=r,
            device_id=(me, side), device_id_type=MESH,
        )
        copy.start()
        pending.append(copy)

    def awaited(ref, s, r):
        pltpu.make_async_remote_copy(
            src_ref=ref, dst_ref=ref, send_sem=s, recv_sem=r, device_id=(me, right), device_id_type=MESH
        ).wait_recv()

    def spread(n, d):
        exchanged(n)
        for g in range(4):
            turned = dot(perm[...], got[n, pl.ds(g * 256, 256), :]).astype(BF16)
            rows = pl.ds(g * 64, 64)
            for c in range(4):
                rows_of[d, h, rows, pl.ds(c * 128, 128)] = turned[c * 64 : (c + 1) * 64]
            mine = rows_of.at[d, h, rows]
            hand(mine, mine, sem_xs.at[d, 0, g], sem_xr.at[d, 0, g], right)
            hand(mine, mine, sem_xs.at[d, 1, g], sem_xr.at[d, 1, g], left)

    def relay(d):
        for g in range(4):
            rows = pl.ds(g * 64, 64)
            from_left, from_right = rows_of.at[d, left, rows], rows_of.at[d, right, rows]
            awaited(from_left, sem_xs.at[d, 0, g], sem_xr.at[d, 0, g])
            if g % 2 == 0:
                hand(from_left, from_left, sem_xs.at[d, 2, g], sem_xr.at[d, 2, g], right)
            awaited(from_right, sem_xs.at[d, 1, g], sem_xr.at[d, 1, g])
            if g % 2 == 1:
                hand(from_right, from_right, sem_xs.at[d, 2, g], sem_xr.at[d, 2, g], left)

    def last_quarter(d):
        for g in range(4):
            awaited(rows_of.at[d, across, pl.ds(g * 64, 64)], sem_xs.at[d, 2, g], sem_xr.at[d, 2, g])

    def gathered(d, use):
        use(h, True)
        relay(d)
        use(left, False)
        use(right, False)
        last_quarter(d)
        use(across, False)

    def go_home(n, d, part):
        upper, lower = pl.ds(0, 128), pl.ds(128, 128)
        for half, side, slot in ((0, right, 0), (1, left, 1)):
            rows = pl.ds(half * 128, 128)
            part_out[d, 0, rows, :] = part(across, half).astype(BF16)
            hand(part_out.at[d, 0, rows], relayed.at[d, slot], sem_ys.at[d, slot], sem_yr.at[d, slot], side)
        part_out[d, 1, lower, :] = part(right, 1).astype(BF16)
        hand(part_out.at[d, 1, lower], summed.at[d, 0, lower], sem_ys.at[d, 2], sem_yr.at[d, 2], right)
        part_out[d, 2, upper, :] = part(left, 0).astype(BF16)
        hand(part_out.at[d, 2, upper], summed.at[d, 1, upper], sem_ys.at[d, 3], sem_yr.at[d, 3], left)
        ahead = part(right, 0)
        awaited(relayed.at[d, 0], sem_ys.at[d, 0], sem_yr.at[d, 0])
        part_out[d, 1, upper, :] = (ahead + relayed[d, 0].astype(F32)).astype(BF16)
        hand(part_out.at[d, 1, upper], summed.at[d, 0, upper], sem_ys.at[d, 4], sem_yr.at[d, 4], right)
        behind = part(left, 1)
        awaited(relayed.at[d, 1], sem_ys.at[d, 1], sem_yr.at[d, 1])
        part_out[d, 2, lower, :] = (behind + relayed[d, 1].astype(F32)).astype(BF16)
        hand(part_out.at[d, 2, lower], summed.at[d, 1, lower], sem_ys.at[d, 5], sem_yr.at[d, 5], left)
        for half in range(2):
            own[pl.ds(half * 128, 128), :] = part(h, half)
        for half in range(2):
            rows = pl.ds(half * 128, 128)
            a, b = (4, 3) if half == 0 else (2, 5)
            awaited(summed.at[d, 0, rows], sem_ys.at[d, a], sem_yr.at[d, a])
            awaited(summed.at[d, 1, rows], sem_ys.at[d, b], sem_yr.at[d, b])
            total = own[rows, :] + summed[d, 0, rows, :].astype(F32) + summed[d, 1, rows, :].astype(F32)
            total = total.astype(BF16)
            for g in (2 * half, 2 * half + 1):
                piece = total[(g % 2) * 64 : (g % 2) * 64 + 64]
                stacked = jnp.concatenate([piece[:, c * 128 : (c + 1) * 128] for c in range(4)], axis=0)
                sent[n, pl.ds(g * 256, 256), :] = dot(perm_t[...], stacked).astype(BF16)
                send_group(n, g, False)
        got[n, 0:16, :] = sent[n, 0:16, :]

    def arrive(n, visit, target):
        exchanged(n)
        back = dot(fetch[visit], got[n])
        for c in range(4):
            target[:, pl.ds(c * 128, 128)] += back[c * 128 : (c + 1) * 128]

    def lift_up(visit):
        def use(k, start):
            a = rows_of[visit, k]
            if start:
                gate[visit] = dot(a, wg[k])
                lift[visit] = dot(a, wu[k])
            else:
                gate[visit] += dot(a, wg[k])
                lift[visit] += dot(a, wu[k])

        gathered(visit, use)
        z = gate[visit]
        hid[visit] = (jax.nn.sigmoid(z) * z * lift[visit]).astype(BF16)

    def put_down(visit):
        def part(k, half):
            return dot(hid[visit, pl.ds(half * 128, 128), :], wd[k])

        return part

    def put_back(k, half):
        rows = pl.ds(half * 128, 128)
        return contract_last(dgate[rows, :], wg[k]) + contract_last(dup[rows, :], wu[k])

    def turn(d, visit):
        def use(k, start):
            value = contract_last(rows_of[d, k], wd[k])
            if start:
                own[:, 0:256] = value
            else:
                own[:, 0:256] += value

        gathered(d, use)
        q, z = own[:, 0:256], gate[visit]
        sigma = jax.nn.sigmoid(z)
        dgate[...] = (q * lift[visit] * sigma * (1.0 + z * (1.0 - sigma))).astype(BF16)
        dup[...] = (q * (z * sigma)).astype(BF16)

    def weigh(d, visit):
        def step(k, carry):
            a, b = rows_of[visit, k], rows_of[d, k]
            by_gate = contract_first(a, dgate[...])
            by_up = contract_first(a, dup[...])
            by_down = contract_first(hid[visit], b)
            if visit < 2:
                by_gate += acc_gate[k]
                by_up += acc_up[k]
                by_down += acc_down[k]
            if visit > 0:
                acc_gate[k] = by_gate
                acc_up[k] = by_up
                acc_down[k] = by_down
            else:
                res_gate[k] = by_gate.astype(BF16)
                res_up[k] = by_up.astype(BF16)
                res_down[k] = by_down.astype(BF16)
            return carry

        lax.fori_loop(0, HIDDEN, step, 0)

    dispatch(0, 0, state[...])
    for load in loads:
        load.wait()
    build(2)
    spread(0, 0)
    dispatch(1, 2, grad[...])
    lift_up(0)
    go_home(2, 0, put_down(0))
    build(1)
    spread(1, 3)
    relay(3)
    arrive(2, 0, state)

    dispatch(3, 1, state[...])
    last_quarter(3)
    spread(3, 1)
    lift_up(1)
    go_home(4, 1, put_down(1))
    arrive(4, 1, state)

    dispatch(5, 2, state[...])
    for k in range(HIDDEN):
        value = contract_last(rows_of[3, k], wd[k])
        if k == 0:
            own[:, 0:256] = value
        else:
            own[:, 0:256] += value
    spread(5, 2)
    lift_up(2)
    q, z = own[:, 0:256], gate[2]
    sigma = jax.nn.sigmoid(z)
    dgate[...] = (q * lift[2] * sigma * (1.0 + z * (1.0 - sigma))).astype(BF16)
    dup[...] = (q * (z * sigma)).astype(BF16)
    go_home(6, 2, put_back)
    weigh(3, 2)
    arrive(6, 2, grad)

    dispatch(7, 1, grad[...])
    spread(7, 4)
    turn(4, 1)
    go_home(8, 3, put_back)
    weigh(4, 1)
    arrive(8, 1, grad)

    dispatch(9, 0, grad[...])
    spread(9, 5)
    turn(5, 0)
    go_home(10, 4, put_back)
    weigh(5, 0)
    stores = [
        pltpu.make_async_copy(res_gate, out_gate, sem_w.at[0]),
        pltpu.make_async_copy(res_up, out_up, sem_w.at[1]),
    ] + [
        pltpu.make_async_copy(res_down.at[k], out_down.at[:, pl.ds(k * 512, 512)], sem_w.at[2 + k])
        for k in range(HIDDEN)
    ]
    for store in stores:
        store.start()
    arrive(10, 0, grad)
    out_tok[...] = grad[...]
    for copy in pending:
        copy.wait_send()
    for store in stores:
        store.wait()


def body(
    tokens, route_first, route_second, route_third, gate_weight, up_weight, down_weight, cotangent
):
    count, width = tokens.shape
    me = lax.axis_index("expert")
    owner = jnp.stack([route[:, 0] for route in (route_first, route_second, route_third)])
    earlier = jnp.arange(count)[None, :] < jnp.arange(count)[:, None]
    same = (owner[:, :, None] == owner[:, None, :]) & earlier[None]
    rank = jnp.sum(same.astype(jnp.int32), axis=2)
    base = lax.rem(owner - me + EXPERTS, EXPERTS) * (4 * RANKS) + rank
    keys = base[:, None, :] + RANKS * jnp.arange(4, dtype=jnp.int32)[None, :, None]
    keys = keys.reshape(3, 4 * count)

    in_vmem = pl.BlockSpec(memory_space=VMEM)
    anywhere = pl.BlockSpec(memory_space=pl.ANY)
    dma = pltpu.SemaphoreType.DMA
    out_tok, out_gate, out_up, out_down = pl.pallas_call(
        kernel,
        out_shape=(
            jax.ShapeDtypeStruct((count, width), F32),
            jax.ShapeDtypeStruct((4, 512, 256), BF16),
            jax.ShapeDtypeStruct((4, 512, 256), BF16),
            jax.ShapeDtypeStruct((256, 2048), BF16),
        ),
        in_specs=[in_vmem] * 4 + [anywhere] * 3,
        out_specs=(in_vmem, anywhere, anywhere, anywhere),
        scratch_shapes=[
            VMEM((4, 512, 256), BF16),
            VMEM((4, 512, 256), BF16),
            VMEM((4, 256, 512), BF16),
            VMEM((3, 1024, 512), BF16),
            VMEM((3, 512, 1024), BF16),
            VMEM((256, 256), BF16),
            VMEM((256, 256), BF16),
            VMEM((11, 1024, 128), BF16),
            VMEM((11, 1024, 128), BF16),
            VMEM((6, 4, 256, 512), BF16),
            VMEM((5, 3, 256, 512), BF16),
            VMEM((5, 2, 128, 512), BF16),
            VMEM((5, 2, 256, 512), BF16),
            VMEM((3, 256, 256), F32),
            VMEM((3, 256, 256), F32),
            VMEM((3, 256, 256), BF16),
            VMEM((256, 256), BF16),
            VMEM((256, 256), BF16),
            VMEM((256, 512), F32),
            VMEM((4, 512, 256), F32),
            VMEM((4, 512, 256), F32),
            VMEM((4, 256, 512), F32),
            VMEM((4, 512, 256), BF16),
            VMEM((4, 512, 256), BF16),
            VMEM((4, 256, 512), BF16),
            VMEM((128, 512), F32),
            VMEM((128, 512), F32),
            dma((6,)),
            dma((11,)),
            dma((11,)),
            dma((6, 3, 4)),
            dma((6, 3, 4)),
            dma((5, 6)),
            dma((5, 6)),
        ],
        compiler_params=pltpu.CompilerParams(
            collective_id=0, has_side_effects=True, vmem_limit_bytes=58 * 2**20
        ),
    )(
        tokens,
        cotangent,
        keys[:, None, :],
        keys[:, :, None],
        gate_weight.reshape(4, 512, 256),
        up_weight.reshape(4, 512, 256),
        down_weight[0],
    )
    return (
        out_tok,
        out_gate.reshape(1, 2048, 256),
        out_up.reshape(1, 2048, 256),
        out_down[None],
    )


def solution(mesh):
    placed = (
        P("expert", "hidden"),
        P("expert", None),
        P("expert", None),
        P("expert", None),
        P("expert", None, "hidden"),
        P("expert", None, "hidden"),
        P("expert", "hidden", None),
        P("expert", "hidden"),
    )
    return jax.shard_map(
        body,
        mesh=mesh,
        in_specs=placed,
        out_specs=(
            P("expert", "hidden"),
            P("expert", None, "hidden"),
            P("expert", None, "hidden"),
            P("expert", "hidden", None),
        ),
        check_vma=False,
    )
```

```python
import jax
import jax.numpy as jnp
from jax import lax
from jax.experimental import pallas as pl
from jax.experimental.pallas import tpu as pltpu
from jax.sharding import PartitionSpec as P

MESH = pl.DeviceIdType.MESH
F32 = jnp.float32
BF16 = jnp.bfloat16
EXPERTS = 64
RANKS = 4
HIDDEN = 4
VMEM = pltpu.VMEM


def dot(a, b):
    return jnp.dot(a, b, preferred_element_type=F32)


def contract_last(a, b):
    return lax.dot_general(a, b, (((1,), (1,)), ((), ())), preferred_element_type=F32)


def contract_first(a, b):
    return lax.dot_general(a, b, (((0,), (0,)), ((), ())), preferred_element_type=F32)


def exact_ones(condition):
    return jnp.where(condition, 1.0, 0.0).astype(BF16)


def near(n, size):
    return lax.rem(((n + 1) // 2) * (2 * lax.rem(n, 2) - 1) + size, size)


def kernel(
    tok, cot, krow, kcol, gate_hbm, up_hbm, down_hbm,
    out_tok, out_gate, out_up, out_down,
    wg, wu, wd, wide, place, fetch, perm, perm_t, sent, got, rows_of, back_rows, q_out, q_in, part_out, part_in,
    gate, lift, hid, dgate, dup, q_own, own, acc_gate, acc_up, acc_down, swap_out, swap_in, state, grad,
    sem_w, sem_send, sem_got, sem_xs, sem_xr, sem_hs, sem_hr, sem_qs, sem_qr, sem_ps, sem_pr, sem_ds, sem_dr,
):
    me = lax.axis_index("expert")
    h = lax.axis_index("hidden")
    y, z, core = me // 16, lax.rem(me // 2, 8), lax.rem(me, 2)
    right, left, across = lax.rem(h + 1, HIDDEN), lax.rem(h + 3, HIDDEN), lax.rem(h + 2, HIDDEN)

    loads = [
        pltpu.make_async_copy(gate_hbm, wg, sem_w.at[0]),
        pltpu.make_async_copy(up_hbm, wu, sem_w.at[1]),
    ] + [
        pltpu.make_async_copy(down_hbm.at[:, pl.ds(k * 512, 512)], wd.at[k], sem_w.at[2 + k])
        for k in range(HIDDEN)
    ]
    for load in loads:
        load.start()

    barrier = pltpu.get_barrier_semaphore()

    def greet(j, carry):
        pl.semaphore_signal(barrier, inc=1, device_id=(lax.rem(me + j, EXPERTS), h), device_id_type=MESH)
        return carry

    lax.fori_loop(1, EXPERTS, greet, 0)
    for o in (1, 2, 3):
        pl.semaphore_signal(barrier, inc=1, device_id=(me, lax.rem(h + o, HIDDEN)), device_id_type=MESH)

    def build(visit):
        def step(g, carry):
            rows = pl.ds(pl.multiple_of(g * 256, 256), 256)
            numbers = lax.broadcasted_iota(jnp.int32, (256, 512), 0) + g * 256
            place[visit, rows, :] = exact_ones(numbers == krow[visit])
            half = pl.ds(pl.multiple_of(g * 128, 128), 128)
            across_lanes = lax.broadcasted_iota(jnp.int32, (128, 1024), 1)
            fetch[visit, half, :] = exact_ones(across_lanes == kcol[visit, half, :])
            return carry

        lax.fori_loop(0, 4, step, 0)

    def image(slot_number):
        c, s = slot_number // 64, slot_number % 64
        return (s // 4) * 16 + c * 4 + s % 4

    first = lax.broadcasted_iota(jnp.int32, (256, 256), 0)
    second = lax.broadcasted_iota(jnp.int32, (256, 256), 1)
    perm[...] = exact_ones(second == image(first))
    perm_t[...] = exact_ones(first == image(second))
    build(0)
    state[...] = tok[...]
    grad[...] = cot[...]
    pl.semaphore_wait(barrier, EXPERTS - 1 + HIDDEN - 1)

    pending = []

    def send_group(n, g, forward):
        def go(t, carry):
            i = g * 16 + 15 - t
            dy, dz, dc = near(i // 16, 4), near(lax.rem(i // 2, 8), 8), lax.rem(i, 2)
            if not forward:
                dy, dz = 4 - dy, 8 - dz
            peer = lax.rem(y + dy, 4) * 16 + lax.rem(z + dz, 8) * 2 + lax.rem(core + dc, 2)
            rows = pl.ds(pl.multiple_of(i * 16, 16), 16)
            pltpu.make_async_remote_copy(
                src_ref=sent.at[n, rows], dst_ref=got.at[n, rows],
                send_sem=sem_send.at[n, g // 2], recv_sem=sem_got.at[n, g // 2],
                device_id=(peer, h), device_id_type=MESH,
            ).start()
            return carry

        lax.fori_loop(0, 16 if g else 15, go, 0)

    def exchanged(n, half):
        rows = pl.ds(16, 31 * 16) if half == 0 else pl.ds(32 * 16, 32 * 16)
        copy = pltpu.make_async_remote_copy(
            src_ref=sent.at[n, rows], dst_ref=got.at[n, rows],
            send_sem=sem_send.at[n, half], recv_sem=sem_got.at[n, half],
            device_id=(lax.rem(me + 1, EXPERTS), h), device_id_type=MESH,
        )
        copy.wait_recv()
        pending.append(copy)

    def stacked(values):
        return jnp.concatenate([values[:, c * 128 : (c + 1) * 128] for c in range(4)], axis=0)

    def dispatch(n, visit, values):
        values = stacked(values.astype(BF16))
        for g in range(4):
            rows = pl.ds(g * 256, 256)
            sent[n, rows, :] = dot(place[visit, rows, :], values).astype(BF16)
            send_group(n, g, True)
        got[n, 0:16, :] = sent[n, 0:16, :]

    def return_rows(n, half, total):
        total = total.astype(BF16)
        for g in (2 * half + 1, 2 * half):
            piece = total[(g % 2) * 64 : (g % 2) * 64 + 64]
            sent[n, pl.ds(g * 256, 256), :] = dot(perm_t[...], stacked(piece)).astype(BF16)
            send_group(n, g, False)
        if half == 0:
            got[n, 0:16, :] = sent[n, 0:16, :]

    def arrive(n, visit, target):
        exchanged(n, 1)
        exchanged(n, 0)
        back = dot(fetch[visit], got[n])
        for c in range(4):
            target[:, pl.ds(c * 128, 128)] += back[c * 128 : (c + 1) * 128]

    def hand(ref_from, ref_to, s, r, side):
        copy = pltpu.make_async_remote_copy(
            src_ref=ref_from, dst_ref=ref_to, send_sem=s, recv_sem=r,
            device_id=(me, side), device_id_type=MESH,
        )
        copy.start()
        pending.append(copy)

    def awaited(ref, s, r):
        pltpu.make_async_remote_copy(
            src_ref=ref, dst_ref=ref, send_sem=s, recv_sem=r, device_id=(me, right), device_id_type=MESH
        ).wait_recv()

    def at_offset(o):
        return lax.rem(h + o, HIDDEN)

    def placed_rows(n, target, g):
        turned = dot(perm[...], got[n, pl.ds(g * 256, 256), :]).astype(BF16)
        for c in range(4):
            target[pl.ds(g * 64, 64), pl.ds(c * 128, 128)] = turned[c * 64 : (c + 1) * 64]

    def spread(n, d):
        for g in range(4):
            if g % 2 == 0:
                exchanged(n, g // 2)
            placed_rows(n, rows_of.at[d, h], g)
            mine = rows_of.at[d, h, pl.ds(g * 64, 64)]
            hand(mine, mine, sem_xs.at[d, 0, g], sem_xr.at[d, 0, g], right)
            hand(mine, mine, sem_xs.at[d, 1, g], sem_xr.at[d, 1, g], left)

    def relay(d):
        for g in range(4):
            rows = pl.ds(g * 64, 64)
            from_left, from_right = rows_of.at[d, left, rows], rows_of.at[d, right, rows]
            awaited(from_left, sem_xs.at[d, 0, g], sem_xr.at[d, 0, g])
            if g % 2 == 0:
                hand(from_left, from_left, sem_xs.at[d, 2, g], sem_xr.at[d, 2, g], right)
            awaited(from_right, sem_xs.at[d, 1, g], sem_xr.at[d, 1, g])
            if g % 2 == 1:
                hand(from_right, from_right, sem_xs.at[d, 2, g], sem_xr.at[d, 2, g], left)

    def lift_up(visit):
        def use(k, start):
            a = rows_of[visit, k]
            if start:
                gate[visit] = dot(a, wg[k])
                lift[visit] = dot(a, wu[k])
            else:
                gate[visit] += dot(a, wg[k])
                lift[visit] += dot(a, wu[k])

        use(h, True)
        relay(visit)
        use(left, False)
        use(right, False)
        for g in range(4):
            awaited(rows_of.at[visit, across, pl.ds(g * 64, 64)], sem_xs.at[visit, 2, g], sem_xr.at[visit, 2, g])
        use(across, False)
        value = gate[visit]
        hid[visit, h] = (jax.nn.sigmoid(value) * value * lift[visit]).astype(BF16)

    def share_hidden(visit):
        for half in (1, 0):
            mine = hid.at[visit, h, pl.ds(half * 128, 128)]
            for o in (2, 1, 3):
                hand(mine, mine, sem_hs.at[visit, o - 1, half], sem_hr.at[visit, o - 1, half], at_offset(o))

    def hidden_shared(visit, half):
        for o in (1, 3, 2):
            ref = hid.at[visit, at_offset(4 - o), pl.ds(half * 128, 128)]
            awaited(ref, sem_hs.at[visit, o - 1, half], sem_hr.at[visit, o - 1, half])

    def put_down(n, visit):
        share_hidden(visit)
        for half in (1, 0):
            hidden_shared(visit, half)
            rows = pl.ds(half * 128, 128)
            total = dot(hid[visit, 0, rows, :], wide[0])
            for k in range(1, HIDDEN):
                total += dot(hid[visit, k, rows, :], wide[k])
            return_rows(n, half, total)

    def collect(n, visit):
        for half in range(2):
            exchanged(n, half)
            for g in (2 * half, 2 * half + 1):
                placed_rows(n, back_rows.at[visit], g)
            rows = pl.ds(half * 128, 128)
            b = back_rows[visit, rows, :]
            for o in (2, 1, 3):
                q_out[visit, o - 1, rows, :] = contract_last(b, wide[at_offset(o)]).astype(BF16)
                hand(
                    q_out.at[visit, o - 1, rows], q_in.at[visit, o - 1, rows],
                    sem_qs.at[visit, o - 1, half], sem_qr.at[visit, o - 1, half], at_offset(o),
                )
            q_own[visit, rows, :] = contract_last(b, wide[h])

    def collected(visit):
        for half in range(2):
            rows = pl.ds(half * 128, 128)
            for o in (1, 3, 2):
                awaited(q_in.at[visit, o - 1, rows], sem_qs.at[visit, o - 1, half], sem_qr.at[visit, o - 1, half])
        q_own[visit] += sum(q_in[visit, o].astype(F32) for o in range(3))

    def derive(visit):
        q, value = q_own[visit], gate[visit]
        sigma = jax.nn.sigmoid(value)
        dgate[...] = (q * lift[visit] * sigma * (1.0 + value * (1.0 - sigma))).astype(BF16)
        dup[...] = (q * (value * sigma)).astype(BF16)

    def put_back(n, visit):
        def part(k, rows):
            return contract_last(dgate[rows, :], wg[k]) + contract_last(dup[rows, :], wu[k])

        for half in (1, 0):
            rows = pl.ds(half * 128, 128)
            for o in (2, 1, 3):
                part_out[visit, o - 1, rows, :] = part(at_offset(o), rows).astype(BF16)
                hand(
                    part_out.at[visit, o - 1, rows], part_in.at[visit, o - 1, rows],
                    sem_ps.at[visit, o - 1, half], sem_pr.at[visit, o - 1, half], at_offset(o),
                )
        for half in (1, 0):
            rows = pl.ds(half * 128, 128)
            own[rows, :] = part(h, rows)
        for half in (1, 0):
            rows = pl.ds(half * 128, 128)
            for o in (1, 3, 2):
                awaited(part_in.at[visit, o - 1, rows], sem_ps.at[visit, o - 1, half], sem_pr.at[visit, o - 1, half])
            total = own[rows, :] + sum(part_in[visit, o, rows, :].astype(F32) for o in range(3))
            return_rows(n, half, total)

    def weigh(visit):
        def step(k, carry):
            a = rows_of[visit, k]
            by_gate = contract_first(a, dgate[...])
            by_up = contract_first(a, dup[...])
            if visit < 2:
                by_gate += acc_gate[k]
                by_up += acc_up[k]
            if visit > 0:
                acc_gate[k] = by_gate
                acc_up[k] = by_up
            else:
                rows = pl.ds(pl.multiple_of(k * 512, 512), 512)
                out_gate[rows, :] = by_gate.astype(BF16)
                out_up[rows, :] = by_up.astype(BF16)
            return carry

        lax.fori_loop(0, HIDDEN, step, 0)

    def weigh_down(visit):
        def step(k, carry):
            by_down = contract_first(hid[visit, k], back_rows[visit])
            if visit < 2:
                by_down += acc_down[k]
            if visit > 0:
                acc_down[k] = by_down
            else:
                swap_out[k] = by_down.astype(BF16)
            return carry

        lax.fori_loop(0, HIDDEN, step, 0)

    dispatch(0, 0, state[...])
    for load in loads:
        load.wait()
    for o in (2, 1, 3):
        hand(wd.at[at_offset(o)], wide.at[h], sem_ds.at[0, o - 1], sem_dr.at[0, o - 1], at_offset(o))
    wide[h] = wd[h]
    build(2)
    spread(0, 0)
    dispatch(1, 2, grad[...])
    lift_up(0)
    for o in (1, 2, 3):
        awaited(wide.at[at_offset(4 - o)], sem_ds.at[0, o - 1], sem_dr.at[0, o - 1])
    put_down(2, 0)
    build(1)
    collect(1, 2)
    arrive(2, 0, state)

    dispatch(3, 1, state[...])
    collected(2)
    spread(3, 1)
    lift_up(1)
    put_down(4, 1)
    arrive(4, 1, state)

    dispatch(5, 2, state[...])
    spread(5, 2)
    lift_up(2)
    derive(2)
    put_back(6, 2)
    share_hidden(2)
    weigh(2)
    arrive(6, 2, grad)

    dispatch(7, 1, grad[...])
    collect(7, 1)
    collected(1)
    derive(1)
    put_back(8, 1)
    for half in range(2):
        hidden_shared(2, half)
    weigh(1)
    weigh_down(2)
    weigh_down(1)
    arrive(8, 1, grad)

    dispatch(9, 0, grad[...])
    collect(9, 0)
    weigh_down(0)
    collected(0)
    derive(0)
    put_back(10, 0)
    for o in (2, 1, 3):
        hand(swap_out.at[at_offset(o)], swap_in.at[h], sem_ds.at[1, o - 1], sem_dr.at[1, o - 1], at_offset(o))
    swap_in[h] = swap_out[h]
    weigh(0)
    arrive(10, 0, grad)
    out_tok[...] = grad[...]
    for o in (1, 2, 3):
        awaited(swap_in.at[at_offset(4 - o)], sem_ds.at[1, o - 1], sem_dr.at[1, o - 1])
    for k in range(HIDDEN):
        out_down[:, pl.ds(k * 512, 512)] = swap_in[k]
    for copy in pending:
        copy.wait_send()


def body(
    tokens, route_first, route_second, route_third, gate_weight, up_weight, down_weight, cotangent
):
    count, width = tokens.shape
    me = lax.axis_index("expert")
    owner = jnp.stack([route[:, 0] for route in (route_first, route_second, route_third)])
    earlier = jnp.arange(count)[None, :] < jnp.arange(count)[:, None]
    same = (owner[:, :, None] == owner[:, None, :]) & earlier[None]
    rank = jnp.sum(same.astype(jnp.int32), axis=2)

    def nearness(there, here, size):
        gap = lax.rem(there - here + size, size)
        return jnp.where(gap == 0, 0, jnp.where(gap <= size // 2, 2 * gap - 1, 2 * (size - gap)))

    position = (
        nearness(owner // 16, me // 16, 4) * 16
        + nearness(lax.rem(owner // 2, 8), lax.rem(me // 2, 8), 8) * 2
        + lax.rem(owner + me, 2)
    )
    base = position * (4 * RANKS) + rank
    keys = base[:, None, :] + RANKS * jnp.arange(4, dtype=jnp.int32)[None, :, None]
    keys = keys.reshape(3, 4 * count)

    in_vmem = pl.BlockSpec(memory_space=VMEM)
    anywhere = pl.BlockSpec(memory_space=pl.ANY)
    dma = pltpu.SemaphoreType.DMA
    results = pl.pallas_call(
        kernel,
        out_shape=(
            jax.ShapeDtypeStruct((count, width), F32),
            jax.ShapeDtypeStruct((2048, 256), BF16),
            jax.ShapeDtypeStruct((2048, 256), BF16),
            jax.ShapeDtypeStruct((256, 2048), BF16),
        ),
        in_specs=[in_vmem] * 4 + [anywhere] * 3,
        out_specs=(in_vmem,) * 4,
        scratch_shapes=[
            VMEM((4, 512, 256), BF16),
            VMEM((4, 512, 256), BF16),
            VMEM((4, 256, 512), BF16),
            VMEM((4, 256, 512), BF16),
            VMEM((3, 1024, 512), BF16),
            VMEM((3, 512, 1024), BF16),
            VMEM((256, 256), BF16),
            VMEM((256, 256), BF16),
            VMEM((11, 1024, 128), BF16),
            VMEM((11, 1024, 128), BF16),
            VMEM((3, 4, 256, 512), BF16),
            VMEM((3, 256, 512), BF16),
            VMEM((3, 3, 256, 256), BF16),
            VMEM((3, 3, 256, 256), BF16),
            VMEM((3, 3, 256, 512), BF16),
            VMEM((3, 3, 256, 512), BF16),
            VMEM((3, 256, 256), F32),
            VMEM((3, 256, 256), F32),
            VMEM((3, 4, 256, 256), BF16),
            VMEM((256, 256), BF16),
            VMEM((256, 256), BF16),
            VMEM((3, 256, 256), F32),
            VMEM((256, 512), F32),
            VMEM((4, 512, 256), F32),
            VMEM((4, 512, 256), F32),
            VMEM((4, 256, 512), F32),
            VMEM((4, 256, 512), BF16),
            VMEM((4, 256, 512), BF16),
            VMEM((128, 512), F32),
            VMEM((128, 512), F32),
            dma((6,)),
            dma((11, 2)),
            dma((11, 2)),
            dma((3, 3, 4)),
            dma((3, 3, 4)),
            dma((3, 3, 2)),
            dma((3, 3, 2)),
            dma((3, 3, 2)),
            dma((3, 3, 2)),
            dma((3, 3, 2)),
            dma((3, 3, 2)),
            dma((2, 3)),
            dma((2, 3)),
        ],
        compiler_params=pltpu.CompilerParams(
            collective_id=0, has_side_effects=True, vmem_limit_bytes=48 * 2**20
        ),
    )(
        tokens,
        cotangent,
        keys[:, None, :],
        keys[:, :, None],
        gate_weight.reshape(4, 512, 256),
        up_weight.reshape(4, 512, 256),
        down_weight[0],
    )
    a, b, c, d = results
    return a, b[None], c[None], d[None]


def solution(mesh):
    placed = (
        P("expert", "hidden"),
        P("expert", None),
        P("expert", None),
        P("expert", None),
        P("expert", None, "hidden"),
        P("expert", None, "hidden"),
        P("expert", "hidden", None),
        P("expert", "hidden"),
    )
    return jax.shard_map(
        body,
        mesh=mesh,
        in_specs=placed,
        out_specs=(
            P("expert", "hidden"),
            P("expert", None, "hidden"),
            P("expert", None, "hidden"),
            P("expert", "hidden", None),
        ),
        check_vma=False,
    )
```

```python
import jax
import jax.numpy as jnp
from jax import lax
from jax.experimental import pallas as pl
from jax.experimental.pallas import tpu as pltpu
from jax.sharding import PartitionSpec as P

MESH = pl.DeviceIdType.MESH
F32 = jnp.float32
BF16 = jnp.bfloat16
EXPERTS = 64
RANKS = 4
HIDDEN = 4
VMEM = pltpu.VMEM


def dot(a, b):
    return jnp.dot(a, b, preferred_element_type=F32)


def contract_last(a, b):
    return lax.dot_general(a, b, (((1,), (1,)), ((), ())), preferred_element_type=F32)


def contract_first(a, b):
    return lax.dot_general(a, b, (((0,), (0,)), ((), ())), preferred_element_type=F32)


def exact_ones(condition):
    return jnp.where(condition, 1.0, 0.0).astype(BF16)


def near(n, size):
    return lax.rem(((n + 1) // 2) * (2 * lax.rem(n, 2) - 1) + size, size)


def kernel(
    tok, cot, krow, kcol, gate_hbm, up_hbm, down_hbm,
    out_tok, out_gate, out_up, out_down,
    wg, wu, wd, wide, place, fetch, perm, perm_t, sent, got, rows_of, back_rows, q_out, q_relayed, q_summed, part_out, relayed, summed,
    gate, lift, hid, dgate, dup, q_own, own, acc_gate, acc_up, acc_down, swap_out, swap_in, state, grad,
    sem_w, sem_send, sem_got, sem_xs, sem_xr, sem_hs, sem_hr, sem_qs, sem_qr, sem_ps, sem_pr, sem_ds, sem_dr,
):
    me = lax.axis_index("expert")
    h = lax.axis_index("hidden")
    y, z, core = me // 16, lax.rem(me // 2, 8), lax.rem(me, 2)
    right, left, across = lax.rem(h + 1, HIDDEN), lax.rem(h + 3, HIDDEN), lax.rem(h + 2, HIDDEN)

    loads = [
        pltpu.make_async_copy(gate_hbm, wg, sem_w.at[0]),
        pltpu.make_async_copy(up_hbm, wu, sem_w.at[1]),
    ] + [
        pltpu.make_async_copy(down_hbm.at[:, pl.ds(k * 512, 512)], wd.at[k], sem_w.at[2 + k])
        for k in range(HIDDEN)
    ]
    for load in loads:
        load.start()

    barrier = pltpu.get_barrier_semaphore()

    def greet(j, carry):
        pl.semaphore_signal(barrier, inc=1, device_id=(lax.rem(me + j, EXPERTS), h), device_id_type=MESH)
        return carry

    lax.fori_loop(1, EXPERTS, greet, 0)
    for o in (1, 2, 3):
        pl.semaphore_signal(barrier, inc=1, device_id=(me, lax.rem(h + o, HIDDEN)), device_id_type=MESH)

    def build(visit):
        def step(g, carry):
            rows = pl.ds(pl.multiple_of(g * 256, 256), 256)
            numbers = lax.broadcasted_iota(jnp.int32, (256, 512), 0) + g * 256
            place[visit, rows, :] = exact_ones(numbers == krow[visit])
            half = pl.ds(pl.multiple_of(g * 128, 128), 128)
            across_lanes = lax.broadcasted_iota(jnp.int32, (128, 1024), 1)
            fetch[visit, half, :] = exact_ones(across_lanes == kcol[visit, half, :])
            return carry

        lax.fori_loop(0, 4, step, 0)

    def image(slot_number):
        c, s = slot_number // 64, slot_number % 64
        return (s // 4) * 16 + c * 4 + s % 4

    first = lax.broadcasted_iota(jnp.int32, (256, 256), 0)
    second = lax.broadcasted_iota(jnp.int32, (256, 256), 1)
    perm[...] = exact_ones(second == image(first))
    perm_t[...] = exact_ones(first == image(second))
    build(0)
    state[...] = tok[...]
    grad[...] = cot[...]
    pl.semaphore_wait(barrier, EXPERTS - 1 + HIDDEN - 1)

    pending = []

    def send_group(n, g, forward):
        def go(t, carry):
            i = g * 16 + 15 - t
            dy, dz, dc = near(i // 16, 4), near(lax.rem(i // 2, 8), 8), lax.rem(i, 2)
            if not forward:
                dy, dz = 4 - dy, 8 - dz
            peer = lax.rem(y + dy, 4) * 16 + lax.rem(z + dz, 8) * 2 + lax.rem(core + dc, 2)
            rows = pl.ds(pl.multiple_of(i * 16, 16), 16)
            pltpu.make_async_remote_copy(
                src_ref=sent.at[n, rows], dst_ref=got.at[n, rows],
                send_sem=sem_send.at[n, g // 2], recv_sem=sem_got.at[n, g // 2],
                device_id=(peer, h), device_id_type=MESH,
            ).start()
            return carry

        lax.fori_loop(0, 16 if g else 15, go, 0)

    def exchanged(n, half):
        rows = pl.ds(16, 31 * 16) if half == 0 else pl.ds(32 * 16, 32 * 16)
        copy = pltpu.make_async_remote_copy(
            src_ref=sent.at[n, rows], dst_ref=got.at[n, rows],
            send_sem=sem_send.at[n, half], recv_sem=sem_got.at[n, half],
            device_id=(lax.rem(me + 1, EXPERTS), h), device_id_type=MESH,
        )
        copy.wait_recv()
        pending.append(copy)

    def stacked(values):
        return jnp.concatenate([values[:, c * 128 : (c + 1) * 128] for c in range(4)], axis=0)

    def dispatch(n, visit, values):
        values = stacked(values.astype(BF16))
        for g in range(4):
            rows = pl.ds(g * 256, 256)
            sent[n, rows, :] = dot(place[visit, rows, :], values).astype(BF16)
            send_group(n, g, True)
        got[n, 0:16, :] = sent[n, 0:16, :]

    def return_rows(n, half, total):
        total = total.astype(BF16)
        for g in (2 * half + 1, 2 * half):
            piece = total[(g % 2) * 64 : (g % 2) * 64 + 64]
            sent[n, pl.ds(g * 256, 256), :] = dot(perm_t[...], stacked(piece)).astype(BF16)
            send_group(n, g, False)
        if half == 0:
            got[n, 0:16, :] = sent[n, 0:16, :]

    def arrive(n, visit, target):
        exchanged(n, 1)
        back = dot(fetch[visit, :, 512:1024], got[n, 512:1024, :])
        exchanged(n, 0)
        back += dot(fetch[visit, :, 0:512], got[n, 0:512, :])
        for c in range(4):
            target[:, pl.ds(c * 128, 128)] += back[c * 128 : (c + 1) * 128]

    def hand(ref_from, ref_to, s, r, side):
        copy = pltpu.make_async_remote_copy(
            src_ref=ref_from, dst_ref=ref_to, send_sem=s, recv_sem=r,
            device_id=(me, side), device_id_type=MESH,
        )
        copy.start()
        pending.append(copy)

    def awaited(ref, s, r):
        pltpu.make_async_remote_copy(
            src_ref=ref, dst_ref=ref, send_sem=s, recv_sem=r, device_id=(me, right), device_id_type=MESH
        ).wait_recv()

    def at_offset(o):
        return lax.rem(h + o, HIDDEN)

    def placed_rows(n, target, g):
        turned = dot(perm[...], got[n, pl.ds(g * 256, 256), :]).astype(BF16)
        for c in range(4):
            target[pl.ds(g * 64, 64), pl.ds(c * 128, 128)] = turned[c * 64 : (c + 1) * 64]

    def spread(n, d):
        for g in range(4):
            if g % 2 == 0:
                exchanged(n, g // 2)
            placed_rows(n, rows_of.at[d, h], g)
            mine = rows_of.at[d, h, pl.ds(g * 64, 64)]
            hand(mine, mine, sem_xs.at[d, 0, g], sem_xr.at[d, 0, g], right)
            hand(mine, mine, sem_xs.at[d, 1, g], sem_xr.at[d, 1, g], left)

    def relay(d):
        for g in range(4):
            rows = pl.ds(g * 64, 64)
            from_left, from_right = rows_of.at[d, left, rows], rows_of.at[d, right, rows]
            awaited(from_left, sem_xs.at[d, 0, g], sem_xr.at[d, 0, g])
            if g % 2 == 0:
                hand(from_left, from_left, sem_xs.at[d, 2, g], sem_xr.at[d, 2, g], right)
            awaited(from_right, sem_xs.at[d, 1, g], sem_xr.at[d, 1, g])
            if g % 2 == 1:
                hand(from_right, from_right, sem_xs.at[d, 2, g], sem_xr.at[d, 2, g], left)

    def in_order(d, use):
        use(h, True)
        relay(d)
        use(left, False)
        use(right, False)
        for g in range(4):
            awaited(rows_of.at[d, across, pl.ds(g * 64, 64)], sem_xs.at[d, 2, g], sem_xr.at[d, 2, g])
        use(across, False)

    def lift_up(visit):
        def use(k, start):
            a = rows_of[visit, k]
            if start:
                gate[visit] = dot(a, wg[k])
                lift[visit] = dot(a, wu[k])
            else:
                gate[visit] += dot(a, wg[k])
                lift[visit] += dot(a, wu[k])

        in_order(visit, use)
        value = gate[visit]
        hid[visit, h] = (jax.nn.sigmoid(value) * value * lift[visit]).astype(BF16)

    def share_hidden(visit):
        for half in (1, 0):
            mine = hid.at[visit, h, pl.ds(half * 128, 128)]
            for o in (2, 1, 3):
                hand(mine, mine, sem_hs.at[visit, o - 1, half], sem_hr.at[visit, o - 1, half], at_offset(o))

    def hidden_shared(visit, half):
        for o in (1, 3, 2):
            ref = hid.at[visit, at_offset(4 - o), pl.ds(half * 128, 128)]
            awaited(ref, sem_hs.at[visit, o - 1, half], sem_hr.at[visit, o - 1, half])

    def put_down(n, visit):
        share_hidden(visit)
        for half in (1, 0):
            hidden_shared(visit, half)
            rows = pl.ds(half * 128, 128)
            total = dot(hid[visit, 0, rows, :], wide[0])
            for k in range(1, HIDDEN):
                total += dot(hid[visit, k, rows, :], wide[k])
            return_rows(n, half, total)

    def over_hidden(order, ready, part, out, passing, arriving, mine, s, r):
        rows = [pl.ds(0, 128), pl.ds(128, 128)]
        for half in order:
            side, other, slot = ((right, left, 2), (left, right, 1))[half]
            ready(half)
            out[0, rows[half], :] = part(across, half).astype(BF16)
            hand(out.at[0, rows[half]], passing.at[half], s.at[half], r.at[half], side)
            out[slot, rows[half], :] = part(other, half).astype(BF16)
            hand(out.at[slot, rows[half]], arriving.at[slot - 1, rows[half]], s.at[2 + half], r.at[2 + half], other)
        for half in order:
            side, slot = ((right, 1), (left, 2))[half]
            value = part(side, half)
            awaited(passing.at[half], s.at[half], r.at[half])
            out[slot, rows[half], :] = (value + passing[half].astype(F32)).astype(BF16)
            hand(out.at[slot, rows[half]], arriving.at[slot - 1, rows[half]], s.at[4 + half], r.at[4 + half], side)
        for half in order:
            mine[rows[half], :] = part(h, half)

    def over_hidden_done(arriving, mine, s, r, half):
        rows = pl.ds(half * 128, 128)
        from_left, from_right = (4, 2) if half == 0 else (3, 5)
        awaited(arriving.at[0, rows], s.at[from_left], r.at[from_left])
        awaited(arriving.at[1, rows], s.at[from_right], r.at[from_right])
        return mine[rows, :] + arriving[0, rows, :].astype(F32) + arriving[1, rows, :].astype(F32)

    def collect(n, visit):
        d = visit - 1

        def ready(half):
            exchanged(n, half)
            for g in (2 * half, 2 * half + 1):
                placed_rows(n, back_rows.at[d], g)

        def part(k, half):
            return contract_last(back_rows[d, pl.ds(half * 128, 128), :], wide[k])

        over_hidden(
            (0, 1), ready, part, q_out.at[d], q_relayed.at[d], q_summed.at[d], q_own.at[visit], sem_qs.at[d], sem_qr.at[d]
        )

    def collected(visit):
        d = visit - 1
        for half in range(2):
            total = over_hidden_done(q_summed.at[d], q_own.at[visit], sem_qs.at[d], sem_qr.at[d], half)
            q_own[visit, pl.ds(half * 128, 128), :] = total

    def collect_whole(n, d):
        spread(n, d)

        def use(k, start):
            value = contract_last(rows_of[d, k], wd[k])
            if start:
                q_own[0] = value
            else:
                q_own[0] += value

        in_order(d, use)

    def derive(visit):
        q, value = q_own[visit], gate[visit]
        sigma = jax.nn.sigmoid(value)
        dgate[...] = (q * lift[visit] * sigma * (1.0 + value * (1.0 - sigma))).astype(BF16)
        dup[...] = (q * (value * sigma)).astype(BF16)

    def put_back(n, visit):
        def part(k, half):
            rows = pl.ds(half * 128, 128)
            return contract_last(dgate[rows, :], wg[k]) + contract_last(dup[rows, :], wu[k])

        over_hidden(
            (1, 0), lambda half: None, part, part_out.at[visit], relayed.at[visit], summed.at[visit], own,
            sem_ps.at[visit], sem_pr.at[visit],
        )
        for half in (1, 0):
            total = over_hidden_done(summed.at[visit], own, sem_ps.at[visit], sem_pr.at[visit], half)
            return_rows(n, half, total)

    def weigh(visit):
        def step(k, carry):
            a = rows_of[visit, k]
            by_gate = contract_first(a, dgate[...])
            by_up = contract_first(a, dup[...])
            if visit < 2:
                by_gate += acc_gate[k]
                by_up += acc_up[k]
            if visit > 0:
                acc_gate[k] = by_gate
                acc_up[k] = by_up
            else:
                rows = pl.ds(pl.multiple_of(k * 512, 512), 512)
                out_gate[rows, :] = by_gate.astype(BF16)
                out_up[rows, :] = by_up.astype(BF16)
            return carry

        lax.fori_loop(0, HIDDEN, step, 0)

    def weigh_down(visit):
        def step(k, carry):
            by_down = contract_first(hid[visit, k], back_rows[visit - 1])
            if visit < 2:
                swap_out[k] = (by_down + acc_down[k]).astype(BF16)
            else:
                acc_down[k] = by_down
            return carry

        lax.fori_loop(0, HIDDEN, step, 0)

    dispatch(0, 0, state[...])
    for load in loads:
        load.wait()
    for o in (2, 1, 3):
        hand(wd.at[at_offset(o)], wide.at[h], sem_ds.at[0, o - 1], sem_dr.at[0, o - 1], at_offset(o))
    wide[h] = wd[h]
    build(2)
    spread(0, 0)
    dispatch(1, 2, grad[...])
    lift_up(0)
    for o in (1, 2, 3):
        awaited(wide.at[at_offset(4 - o)], sem_ds.at[0, o - 1], sem_dr.at[0, o - 1])
    put_down(2, 0)
    build(1)
    collect(1, 2)
    arrive(2, 0, state)

    dispatch(3, 1, state[...])
    collected(2)
    spread(3, 1)
    lift_up(1)
    put_down(4, 1)
    arrive(4, 1, state)

    dispatch(5, 2, state[...])
    spread(5, 2)
    lift_up(2)
    derive(2)
    put_back(6, 2)
    share_hidden(2)
    weigh(2)
    arrive(6, 2, grad)

    dispatch(7, 1, grad[...])
    collect(7, 1)
    collected(1)
    derive(1)
    put_back(8, 1)
    for half in range(2):
        hidden_shared(2, half)
    weigh(1)
    weigh_down(2)
    weigh_down(1)
    for o in (2, 1, 3):
        hand(swap_out.at[at_offset(o)], swap_in.at[h], sem_ds.at[1, o - 1], sem_dr.at[1, o - 1], at_offset(o))
    swap_in[h] = swap_out[h]
    arrive(8, 1, grad)

    dispatch(9, 0, grad[...])
    collect_whole(9, 3)
    derive(0)
    put_back(10, 0)
    weigh(0)
    for o in (1, 2, 3):
        awaited(swap_in.at[at_offset(4 - o)], sem_ds.at[1, o - 1], sem_dr.at[1, o - 1])
    for k in range(HIDDEN):
        by_down = contract_first(hid[0, h], rows_of[3, k]) + swap_in[k].astype(F32)
        out_down[:, pl.ds(k * 512, 512)] = by_down.astype(BF16)
    arrive(10, 0, grad)
    out_tok[...] = grad[...]
    for copy in pending:
        copy.wait_send()


def body(
    tokens, route_first, route_second, route_third, gate_weight, up_weight, down_weight, cotangent
):
    count, width = tokens.shape
    me = lax.axis_index("expert")
    owner = jnp.stack([route[:, 0] for route in (route_first, route_second, route_third)])
    earlier = jnp.arange(count)[None, :] < jnp.arange(count)[:, None]
    same = (owner[:, :, None] == owner[:, None, :]) & earlier[None]
    rank = jnp.sum(same.astype(jnp.int32), axis=2)

    def nearness(there, here, size):
        gap = lax.rem(there - here + size, size)
        return jnp.where(gap == 0, 0, jnp.where(gap <= size // 2, 2 * gap - 1, 2 * (size - gap)))

    position = (
        nearness(owner // 16, me // 16, 4) * 16
        + nearness(lax.rem(owner // 2, 8), lax.rem(me // 2, 8), 8) * 2
        + lax.rem(owner + me, 2)
    )
    base = position * (4 * RANKS) + rank
    keys = base[:, None, :] + RANKS * jnp.arange(4, dtype=jnp.int32)[None, :, None]
    keys = keys.reshape(3, 4 * count)

    in_vmem = pl.BlockSpec(memory_space=VMEM)
    anywhere = pl.BlockSpec(memory_space=pl.ANY)
    dma = pltpu.SemaphoreType.DMA
    results = pl.pallas_call(
        kernel,
        out_shape=(
            jax.ShapeDtypeStruct((count, width), F32),
            jax.ShapeDtypeStruct((2048, 256), BF16),
            jax.ShapeDtypeStruct((2048, 256), BF16),
            jax.ShapeDtypeStruct((256, 2048), BF16),
        ),
        in_specs=[in_vmem] * 4 + [anywhere] * 3,
        out_specs=(in_vmem,) * 4,
        scratch_shapes=[
            VMEM((4, 512, 256), BF16),
            VMEM((4, 512, 256), BF16),
            VMEM((4, 256, 512), BF16),
            VMEM((4, 256, 512), BF16),
            VMEM((3, 1024, 512), BF16),
            VMEM((3, 512, 1024), BF16),
            VMEM((256, 256), BF16),
            VMEM((256, 256), BF16),
            VMEM((11, 1024, 128), BF16),
            VMEM((11, 1024, 128), BF16),
            VMEM((4, 4, 256, 512), BF16),
            VMEM((2, 256, 512), BF16),
            VMEM((2, 3, 256, 256), BF16),
            VMEM((2, 2, 128, 256), BF16),
            VMEM((2, 2, 256, 256), BF16),
            VMEM((3, 3, 256, 512), BF16),
            VMEM((3, 2, 128, 512), BF16),
            VMEM((3, 2, 256, 512), BF16),
            VMEM((3, 256, 256), F32),
            VMEM((3, 256, 256), F32),
            VMEM((3, 4, 256, 256), BF16),
            VMEM((256, 256), BF16),
            VMEM((256, 256), BF16),
            VMEM((3, 256, 256), F32),
            VMEM((256, 512), F32),
            VMEM((4, 512, 256), F32),
            VMEM((4, 512, 256), F32),
            VMEM((4, 256, 512), F32),
            VMEM((4, 256, 512), BF16),
            VMEM((4, 256, 512), BF16),
            VMEM((128, 512), F32),
            VMEM((128, 512), F32),
            dma((6,)),
            dma((11, 2)),
            dma((11, 2)),
            dma((4, 3, 4)),
            dma((4, 3, 4)),
            dma((3, 3, 2)),
            dma((3, 3, 2)),
            dma((2, 6)),
            dma((2, 6)),
            dma((3, 6)),
            dma((3, 6)),
            dma((2, 3)),
            dma((2, 3)),
        ],
        compiler_params=pltpu.CompilerParams(
            collective_id=0, has_side_effects=True, vmem_limit_bytes=48 * 2**20
        ),
    )(
        tokens,
        cotangent,
        keys[:, None, :],
        keys[:, :, None],
        gate_weight.reshape(4, 512, 256),
        up_weight.reshape(4, 512, 256),
        down_weight[0],
    )
    a, b, c, d = results
    return a, b[None], c[None], d[None]


def solution(mesh):
    placed = (
        P("expert", "hidden"),
        P("expert", None),
        P("expert", None),
        P("expert", None),
        P("expert", None, "hidden"),
        P("expert", None, "hidden"),
        P("expert", "hidden", None),
        P("expert", "hidden"),
    )
    return jax.shard_map(
        body,
        mesh=mesh,
        in_specs=placed,
        out_specs=(
            P("expert", "hidden"),
            P("expert", None, "hidden"),
            P("expert", None, "hidden"),
            P("expert", "hidden", None),
        ),
        check_vma=False,
    )
```

```python
import jax
import jax.numpy as jnp
from jax import lax
from jax.experimental import pallas as pl
from jax.experimental.pallas import tpu as pltpu
from jax.sharding import PartitionSpec as P

MESH = pl.DeviceIdType.MESH
F32 = jnp.float32
BF16 = jnp.bfloat16
EXPERTS = 64
RANKS = 4
HIDDEN = 4
VMEM = pltpu.VMEM


def dot(a, b):
    return jnp.dot(a, b, preferred_element_type=F32)


def contract_last(a, b):
    return lax.dot_general(a, b, (((1,), (1,)), ((), ())), preferred_element_type=F32)


def contract_first(a, b):
    return lax.dot_general(a, b, (((0,), (0,)), ((), ())), preferred_element_type=F32)


def exact_ones(condition):
    return jnp.where(condition, 1.0, 0.0).astype(BF16)


def near(n, size):
    return lax.rem(((n + 1) // 2) * (2 * lax.rem(n, 2) - 1) + size, size)


def kernel(
    tok, cot, route_0, route_1, route_2, gate_hbm, up_hbm, down_hbm,
    out_tok, out_gate, out_up, out_down,
    krow, kcol, wg, wu, wd, wide, place, fetch, perm, perm_t, sent, got, rows_of, back_rows, q_out, q_relayed, q_summed, part_out, relayed, summed,
    gate, lift, hid, dgate, dup, q_own, own, acc_gate, acc_up, acc_down, swap_out, swap_in, state, grad,
    sem_w, sem_send, sem_got, sem_xs, sem_xr, sem_hs, sem_hr, sem_qs, sem_qr, sem_ps, sem_pr, sem_ds, sem_dr,
):
    me = lax.axis_index("expert")
    h = lax.axis_index("hidden")
    y, z, core = me // 16, lax.rem(me // 2, 8), lax.rem(me, 2)
    right, left, across = lax.rem(h + 1, HIDDEN), lax.rem(h + 3, HIDDEN), lax.rem(h + 2, HIDDEN)

    loads = [
        pltpu.make_async_copy(gate_hbm, wg, sem_w.at[0]),
        pltpu.make_async_copy(up_hbm, wu, sem_w.at[1]),
    ] + [
        pltpu.make_async_copy(down_hbm.at[:, pl.ds(k * 512, 512)], wd.at[k], sem_w.at[2 + k])
        for k in range(HIDDEN)
    ]
    for load in loads:
        load.start()
    starts = [
        pltpu.make_async_copy(tok, state, sem_w.at[6]),
        pltpu.make_async_copy(cot, grad, sem_w.at[7]),
    ]
    for start in starts:
        start.start()

    barrier = pltpu.get_barrier_semaphore()

    def greet(j, carry):
        pl.semaphore_signal(barrier, inc=1, device_id=(lax.rem(me + j, EXPERTS), h), device_id_type=MESH)
        return carry

    lax.fori_loop(1, EXPERTS, greet, 0)
    for o in (1, 2, 3):
        pl.semaphore_signal(barrier, inc=1, device_id=(me, lax.rem(h + o, HIDDEN)), device_id_type=MESH)

    def nearness(gap, size):
        return jnp.where(gap == 0, 0, jnp.where(gap <= size // 2, 2 * gap - 1, 2 * (size - gap)))

    def keys_of(owner, rank):
        gap_y = jnp.bitwise_and(jnp.right_shift(owner, 4) - y + 4, 3)
        gap_z = jnp.bitwise_and(jnp.right_shift(owner, 1) - z + 8, 7)
        gap_core = jnp.bitwise_and(owner + core, 1)
        return (nearness(gap_y, 4) * 16 + nearness(gap_z, 8) * 2 + gap_core) * (4 * RANKS) + rank

    def build(visit):
        along = jnp.broadcast_to((route_0, route_1, route_2)[visit][...].astype(F32), (128, 128))
        down = jnp.transpose(along)
        token = lax.broadcasted_iota(jnp.int32, (128, 128), 0)
        other = lax.broadcasted_iota(jnp.int32, (128, 128), 1)
        same = along == down
        rank_down = jnp.sum(jnp.where(same & (other < token), 1.0, 0.0), axis=1, keepdims=True)
        rank_along = jnp.sum(jnp.where(same & (token < other), 1.0, 0.0), axis=0, keepdims=True)
        key_along = keys_of(along[0:1, :].astype(jnp.int32), rank_along.astype(jnp.int32))
        key_down = keys_of(down[:, 0:1].astype(jnp.int32), rank_down.astype(jnp.int32))
        for c in range(4):
            krow[visit, :, pl.ds(c * 128, 128)] = key_along + RANKS * c
            kcol[visit, pl.ds(c * 128, 128), :] = key_down + RANKS * c

        def step(g, carry):
            rows = pl.ds(pl.multiple_of(g * 256, 256), 256)
            numbers = lax.broadcasted_iota(jnp.int32, (256, 512), 0) + g * 256
            place[visit, rows, :] = exact_ones(numbers == krow[visit])
            half = pl.ds(pl.multiple_of(g * 128, 128), 128)
            across_lanes = lax.broadcasted_iota(jnp.int32, (128, 1024), 1)
            fetch[visit, half, :] = exact_ones(across_lanes == kcol[visit, half, :])
            return carry

        lax.fori_loop(0, 4, step, 0)

    def image(slot_number):
        c, s = slot_number // 64, slot_number % 64
        return (s // 4) * 16 + c * 4 + s % 4

    first = lax.broadcasted_iota(jnp.int32, (256, 256), 0)
    second = lax.broadcasted_iota(jnp.int32, (256, 256), 1)
    perm[...] = exact_ones(second == image(first))
    perm_t[...] = exact_ones(first == image(second))
    build(0)
    pl.semaphore_wait(barrier, EXPERTS - 1 + HIDDEN - 1)

    pending = []

    def send_group(n, g, forward):
        def go(t, carry):
            i = g * 16 + 15 - t
            dy, dz, dc = near(i // 16, 4), near(lax.rem(i // 2, 8), 8), lax.rem(i, 2)
            if not forward:
                dy, dz = 4 - dy, 8 - dz
            peer = lax.rem(y + dy, 4) * 16 + lax.rem(z + dz, 8) * 2 + lax.rem(core + dc, 2)
            rows = pl.ds(pl.multiple_of(i * 16, 16), 16)
            pltpu.make_async_remote_copy(
                src_ref=sent.at[n, rows], dst_ref=got.at[n, rows],
                send_sem=sem_send.at[n, g // 2], recv_sem=sem_got.at[n, g // 2],
                device_id=(peer, h), device_id_type=MESH,
            ).start()
            return carry

        lax.fori_loop(0, 16 if g else 15, go, 0)

    def exchanged(n, half):
        rows = pl.ds(16, 31 * 16) if half == 0 else pl.ds(32 * 16, 32 * 16)
        copy = pltpu.make_async_remote_copy(
            src_ref=sent.at[n, rows], dst_ref=got.at[n, rows],
            send_sem=sem_send.at[n, half], recv_sem=sem_got.at[n, half],
            device_id=(lax.rem(me + 1, EXPERTS), h), device_id_type=MESH,
        )
        copy.wait_recv()
        pending.append(copy)

    def stacked(values):
        return jnp.concatenate([values[:, c * 128 : (c + 1) * 128] for c in range(4)], axis=0)

    def dispatch(n, visit, values):
        values = stacked(values.astype(BF16))
        for g in range(4):
            rows = pl.ds(g * 256, 256)
            sent[n, rows, :] = dot(place[visit, rows, :], values).astype(BF16)
            send_group(n, g, True)
        got[n, 0:16, :] = sent[n, 0:16, :]

    def return_rows(n, half, total):
        total = total.astype(BF16)
        for g in (2 * half + 1, 2 * half):
            piece = total[(g % 2) * 64 : (g % 2) * 64 + 64]
            sent[n, pl.ds(g * 256, 256), :] = dot(perm_t[...], stacked(piece)).astype(BF16)
            send_group(n, g, False)
        if half == 0:
            got[n, 0:16, :] = sent[n, 0:16, :]

    def arrive(n, visit, target):
        exchanged(n, 1)
        back = dot(fetch[visit, :, 512:1024], got[n, 512:1024, :])
        exchanged(n, 0)
        back += dot(fetch[visit, :, 0:512], got[n, 0:512, :])
        for c in range(4):
            target[:, pl.ds(c * 128, 128)] += back[c * 128 : (c + 1) * 128]

    def hand(ref_from, ref_to, s, r, side):
        copy = pltpu.make_async_remote_copy(
            src_ref=ref_from, dst_ref=ref_to, send_sem=s, recv_sem=r,
            device_id=(me, side), device_id_type=MESH,
        )
        copy.start()
        pending.append(copy)

    def awaited(ref, s, r):
        pltpu.make_async_remote_copy(
            src_ref=ref, dst_ref=ref, send_sem=s, recv_sem=r, device_id=(me, right), device_id_type=MESH
        ).wait_recv()

    def at_offset(o):
        return lax.rem(h + o, HIDDEN)

    def placed_rows(n, target, g):
        turned = dot(perm[...], got[n, pl.ds(g * 256, 256), :]).astype(BF16)
        for c in range(4):
            target[pl.ds(g * 64, 64), pl.ds(c * 128, 128)] = turned[c * 64 : (c + 1) * 64]

    def spread(n, d):
        for g in range(4):
            if g % 2 == 0:
                exchanged(n, g // 2)
            placed_rows(n, rows_of.at[d, h], g)
            mine = rows_of.at[d, h, pl.ds(g * 64, 64)]
            hand(mine, mine, sem_xs.at[d, 0, g], sem_xr.at[d, 0, g], right)
            hand(mine, mine, sem_xs.at[d, 1, g], sem_xr.at[d, 1, g], left)

    def relay(d):
        for g in range(4):
            rows = pl.ds(g * 64, 64)
            from_left, from_right = rows_of.at[d, left, rows], rows_of.at[d, right, rows]
            awaited(from_left, sem_xs.at[d, 0, g], sem_xr.at[d, 0, g])
            if g % 2 == 0:
                hand(from_left, from_left, sem_xs.at[d, 2, g], sem_xr.at[d, 2, g], right)
            awaited(from_right, sem_xs.at[d, 1, g], sem_xr.at[d, 1, g])
            if g % 2 == 1:
                hand(from_right, from_right, sem_xs.at[d, 2, g], sem_xr.at[d, 2, g], left)

    def in_order(d, use):
        use(h, True)
        relay(d)
        use(left, False)
        use(right, False)
        for g in range(4):
            awaited(rows_of.at[d, across, pl.ds(g * 64, 64)], sem_xs.at[d, 2, g], sem_xr.at[d, 2, g])
        use(across, False)

    def lift_up(visit):
        def use(k, start):
            a = rows_of[visit, k]
            if start:
                gate[visit] = dot(a, wg[k])
                lift[visit] = dot(a, wu[k])
            else:
                gate[visit] += dot(a, wg[k])
                lift[visit] += dot(a, wu[k])

        in_order(visit, use)
        value = gate[visit]
        hid[visit, h] = (jax.nn.sigmoid(value) * value * lift[visit]).astype(BF16)

    def share_hidden(visit):
        for half in (1, 0):
            mine = hid.at[visit, h, pl.ds(half * 128, 128)]
            for o in (2, 1, 3):
                hand(mine, mine, sem_hs.at[visit, o - 1, half], sem_hr.at[visit, o - 1, half], at_offset(o))

    def hidden_shared(visit, half):
        for o in (1, 3, 2):
            ref = hid.at[visit, at_offset(4 - o), pl.ds(half * 128, 128)]
            awaited(ref, sem_hs.at[visit, o - 1, half], sem_hr.at[visit, o - 1, half])

    def put_down(n, visit):
        share_hidden(visit)
        for half in (1, 0):
            hidden_shared(visit, half)
            rows = pl.ds(half * 128, 128)
            total = dot(hid[visit, 0, rows, :], wide[0])
            for k in range(1, HIDDEN):
                total += dot(hid[visit, k, rows, :], wide[k])
            return_rows(n, half, total)

    def over_hidden(order, ready, part, out, passing, arriving, mine, s, r):
        rows = [pl.ds(0, 128), pl.ds(128, 128)]
        for half in order:
            side, other, slot = ((right, left, 2), (left, right, 1))[half]
            ready(half)
            out[0, rows[half], :] = part(across, half).astype(BF16)
            hand(out.at[0, rows[half]], passing.at[half], s.at[half], r.at[half], side)
            out[slot, rows[half], :] = part(other, half).astype(BF16)
            hand(out.at[slot, rows[half]], arriving.at[slot - 1, rows[half]], s.at[2 + half], r.at[2 + half], other)
        for half in order:
            side, slot = ((right, 1), (left, 2))[half]
            value = part(side, half)
            awaited(passing.at[half], s.at[half], r.at[half])
            out[slot, rows[half], :] = (value + passing[half].astype(F32)).astype(BF16)
            hand(out.at[slot, rows[half]], arriving.at[slot - 1, rows[half]], s.at[4 + half], r.at[4 + half], side)
        for half in order:
            mine[rows[half], :] = part(h, half)

    def over_hidden_done(arriving, mine, s, r, half):
        rows = pl.ds(half * 128, 128)
        from_left, from_right = (4, 2) if half == 0 else (3, 5)
        awaited(arriving.at[0, rows], s.at[from_left], r.at[from_left])
        awaited(arriving.at[1, rows], s.at[from_right], r.at[from_right])
        return mine[rows, :] + arriving[0, rows, :].astype(F32) + arriving[1, rows, :].astype(F32)

    def collect(n, visit):
        d = visit - 1

        def ready(half):
            exchanged(n, half)
            for g in (2 * half, 2 * half + 1):
                placed_rows(n, back_rows.at[d], g)

        def part(k, half):
            return contract_last(back_rows[d, pl.ds(half * 128, 128), :], wide[k])

        over_hidden(
            (0, 1), ready, part, q_out.at[d], q_relayed.at[d], q_summed.at[d], q_own.at[visit], sem_qs.at[d], sem_qr.at[d]
        )

    def collected(visit):
        d = visit - 1
        for half in range(2):
            total = over_hidden_done(q_summed.at[d], q_own.at[visit], sem_qs.at[d], sem_qr.at[d], half)
            q_own[visit, pl.ds(half * 128, 128), :] = total

    def collect_whole(n, d):
        spread(n, d)

        def use(k, start):
            value = contract_last(rows_of[d, k], wd[k])
            if start:
                q_own[0] = value
            else:
                q_own[0] += value

        in_order(d, use)

    def derive(visit):
        q, value = q_own[visit], gate[visit]
        sigma = jax.nn.sigmoid(value)
        dgate[...] = (q * lift[visit] * sigma * (1.0 + value * (1.0 - sigma))).astype(BF16)
        dup[...] = (q * (value * sigma)).astype(BF16)

    def put_back(n, visit):
        def part(k, half):
            rows = pl.ds(half * 128, 128)
            return contract_last(dgate[rows, :], wg[k]) + contract_last(dup[rows, :], wu[k])

        over_hidden(
            (1, 0), lambda half: None, part, part_out.at[visit], relayed.at[visit], summed.at[visit], own,
            sem_ps.at[visit], sem_pr.at[visit],
        )
        for half in (1, 0):
            total = over_hidden_done(summed.at[visit], own, sem_ps.at[visit], sem_pr.at[visit], half)
            return_rows(n, half, total)

    def weigh(visit):
        def step(k, carry):
            a = rows_of[visit, k]
            by_gate = contract_first(a, dgate[...])
            by_up = contract_first(a, dup[...])
            if visit < 2:
                by_gate += acc_gate[k]
                by_up += acc_up[k]
            if visit > 0:
                acc_gate[k] = by_gate
                acc_up[k] = by_up
            else:
                rows = pl.ds(pl.multiple_of(k * 512, 512), 512)
                out_gate[rows, :] = by_gate.astype(BF16)
                out_up[rows, :] = by_up.astype(BF16)
            return carry

        lax.fori_loop(0, HIDDEN, step, 0)

    def weigh_down(visit):
        def step(k, carry):
            by_down = contract_first(hid[visit, k], back_rows[visit - 1])
            if visit < 2:
                swap_out[k] = (by_down + acc_down[k]).astype(BF16)
            else:
                acc_down[k] = by_down
            return carry

        lax.fori_loop(0, HIDDEN, step, 0)

    for load in loads + starts:
        load.wait()
    for o in (2, 1, 3):
        hand(wd.at[at_offset(o)], wide.at[h], sem_ds.at[0, o - 1], sem_dr.at[0, o - 1], at_offset(o))
    dispatch(0, 0, state[...])
    wide[h] = wd[h]
    build(2)
    spread(0, 0)
    dispatch(1, 2, grad[...])
    lift_up(0)
    for o in (1, 2, 3):
        awaited(wide.at[at_offset(4 - o)], sem_ds.at[0, o - 1], sem_dr.at[0, o - 1])
    put_down(2, 0)
    build(1)
    collect(1, 2)
    arrive(2, 0, state)

    dispatch(3, 1, state[...])
    collected(2)
    spread(3, 1)
    lift_up(1)
    put_down(4, 1)
    arrive(4, 1, state)

    dispatch(5, 2, state[...])
    spread(5, 2)
    lift_up(2)
    derive(2)
    put_back(6, 2)
    share_hidden(2)
    weigh(2)
    arrive(6, 2, grad)

    dispatch(7, 1, grad[...])
    collect(7, 1)
    collected(1)
    derive(1)
    put_back(8, 1)
    for half in range(2):
        hidden_shared(2, half)
    weigh(1)
    weigh_down(2)
    weigh_down(1)
    for o in (2, 1, 3):
        hand(swap_out.at[at_offset(o)], swap_in.at[h], sem_ds.at[1, o - 1], sem_dr.at[1, o - 1], at_offset(o))
    swap_in[h] = swap_out[h]
    arrive(8, 1, grad)

    dispatch(9, 0, grad[...])
    collect_whole(9, 3)
    derive(0)
    put_back(10, 0)
    weigh(0)
    for o in (1, 2, 3):
        awaited(swap_in.at[at_offset(4 - o)], sem_ds.at[1, o - 1], sem_dr.at[1, o - 1])
    for k in range(HIDDEN):
        by_down = contract_first(hid[0, h], rows_of[3, k]) + swap_in[k].astype(F32)
        out_down[:, pl.ds(k * 512, 512)] = by_down.astype(BF16)
    arrive(10, 0, grad)
    out_tok[...] = grad[...]
    for copy in pending:
        copy.wait_send()


def body(
    tokens, route_first, route_second, route_third, gate_weight, up_weight, down_weight, cotangent
):
    count, width = tokens.shape
    in_vmem = pl.BlockSpec(memory_space=VMEM)
    in_hbm = pl.BlockSpec(memory_space=pltpu.HBM)
    dma = pltpu.SemaphoreType.DMA
    results = pl.pallas_call(
        kernel,
        out_shape=(
            jax.ShapeDtypeStruct((count, width), F32),
            jax.ShapeDtypeStruct((2048, 256), BF16),
            jax.ShapeDtypeStruct((2048, 256), BF16),
            jax.ShapeDtypeStruct((256, 2048), BF16),
        ),
        in_specs=[in_hbm] * 2 + [in_vmem] * 3 + [in_hbm] * 3,
        out_specs=(in_vmem,) * 4,
        scratch_shapes=[
            VMEM((3, 1, 512), jnp.int32),
            VMEM((3, 512, 1), jnp.int32),
            VMEM((4, 512, 256), BF16),
            VMEM((4, 512, 256), BF16),
            VMEM((4, 256, 512), BF16),
            VMEM((4, 256, 512), BF16),
            VMEM((3, 1024, 512), BF16),
            VMEM((3, 512, 1024), BF16),
            VMEM((256, 256), BF16),
            VMEM((256, 256), BF16),
            VMEM((11, 1024, 128), BF16),
            VMEM((11, 1024, 128), BF16),
            VMEM((4, 4, 256, 512), BF16),
            VMEM((2, 256, 512), BF16),
            VMEM((2, 3, 256, 256), BF16),
            VMEM((2, 2, 128, 256), BF16),
            VMEM((2, 2, 256, 256), BF16),
            VMEM((3, 3, 256, 512), BF16),
            VMEM((3, 2, 128, 512), BF16),
            VMEM((3, 2, 256, 512), BF16),
            VMEM((3, 256, 256), F32),
            VMEM((3, 256, 256), F32),
            VMEM((3, 4, 256, 256), BF16),
            VMEM((256, 256), BF16),
            VMEM((256, 256), BF16),
            VMEM((3, 256, 256), F32),
            VMEM((256, 512), F32),
            VMEM((4, 512, 256), F32),
            VMEM((4, 512, 256), F32),
            VMEM((4, 256, 512), F32),
            VMEM((4, 256, 512), BF16),
            VMEM((4, 256, 512), BF16),
            VMEM((128, 512), F32),
            VMEM((128, 512), F32),
            dma((8,)),
            dma((11, 2)),
            dma((11, 2)),
            dma((4, 3, 4)),
            dma((4, 3, 4)),
            dma((3, 3, 2)),
            dma((3, 3, 2)),
            dma((2, 6)),
            dma((2, 6)),
            dma((3, 6)),
            dma((3, 6)),
            dma((2, 3)),
            dma((2, 3)),
        ],
        compiler_params=pltpu.CompilerParams(
            collective_id=0, has_side_effects=True, vmem_limit_bytes=54 * 2**20
        ),
    )(
        tokens,
        cotangent,
        route_first.reshape(1, count),
        route_second.reshape(1, count),
        route_third.reshape(1, count),
        gate_weight.reshape(4, 512, 256),
        up_weight.reshape(4, 512, 256),
        down_weight[0],
    )
    a, b, c, d = results
    return a, b[None], c[None], d[None]


def solution(mesh):
    placed = (
        P("expert", "hidden"),
        P("expert", None),
        P("expert", None),
        P("expert", None),
        P("expert", None, "hidden"),
        P("expert", None, "hidden"),
        P("expert", "hidden", None),
        P("expert", "hidden"),
    )
    return jax.shard_map(
        body,
        mesh=mesh,
        in_specs=placed,
        out_specs=(
            P("expert", "hidden"),
            P("expert", None, "hidden"),
            P("expert", None, "hidden"),
            P("expert", "hidden", None),
        ),
        check_vma=False,
    )
```
